32 devices in a mesh: dp: 8 (over z, y), tensor: 4 (over x, core).
Axes of the slice: x: 2, y: 2, z: 4, core: 2. Of those that a mesh axis runs over, the one named last changes fastest.
Arguments:
- tokens: bfloat16 [8192, 768], P(('dp', 'tensor')), may hold values from -6 to 6
- gain_attn: bfloat16 [768], P('dp'), may hold values from 0.5 to 1.5
- gain_mlp: bfloat16 [768], P('dp'), may hold values from 0.5 to 1.5
- w_qkv: bfloat16 [3, 768, 768], P(None, 'dp', 'tensor'), may hold values from -0.3125 to 0.3125
- w_out: bfloat16 [768, 768], P('tensor', 'dp'), may hold values from -0.875 to 0.875
- w_in: bfloat16 [2, 768, 1152], P(None, 'dp', 'tensor'), may hold values from -0.21875 to 0.21875
- w_down: bfloat16 [1152, 768], P('tensor', 'dp'), may hold values from -0.1875 to 0.1875
- cotangent: bfloat16 [8192, 768], P(('dp', 'tensor')), may hold values from -6 to 6
Outputs:
- mixed: bfloat16 [8192, 768], P(('dp', 'tensor'))
- input_grad: float32 [8192, 768], P(('dp', 'tensor'))
- grad_gain_attn: float32 [768], P('dp')
- grad_gain_mlp: float32 [768], P('dp')
- grad_qkv: float32 [3, 768, 768], P(None, 'dp', 'tensor')
- grad_out: float32 [768, 768], P('tensor', 'dp')
- grad_in: float32 [2, 768, 1152], P(None, 'dp', 'tensor')
- grad_down: float32 [1152, 768], P('tensor', 'dp')
The draws below stay inside these ranges and needn't reach their ends.
All inputs are finite; a program needn't handle non-finite values.
Results may differ from the reference program's by a relative error of at most 0.018.
The reference program's roundings to bfloat16 on the way count: a program that leaves them out, or rounds other values in their place, can miss the bound.
Values may be sent and summed in bfloat16 or wider, within the bound.
A program may use at most 128 MiB of HBM per device.

```python
import jax
import jax.numpy as jnp
from jax import lax

D = 768
HEADS = 12
HEAD = 64
FF = 1152
LEN = 1024
TOKENS = 8192


def with_spikes(array, own_key, source, target, parts, factor):
    owner, partner = [(jnp.arange(array.shape[position]) // (array.shape[position] // parts)).reshape([-1 if axis == position else 1 for axis in range(array.ndim)]) for position in (source, target)]
    chosen = jax.random.permutation(own_key, parts)[partner]
    strong = (owner == chosen) | (owner == (partner + parts // 2) % parts)
    return jnp.where(strong, factor * array, array)


def block_scale(rng, extent, split, smallest, largest):
    factor_of = 1.0
    for axis_at, parts in split:
        steps = jax.random.uniform(jax.random.fold_in(jax.random.fold_in(rng, 6), axis_at), (parts,), jnp.float32, smallest / len(split), largest / len(split))
        factor_of = factor_of * jnp.repeat(jnp.exp(steps), extent[axis_at] // parts).reshape((-1,) + (1,) * (len(extent) - 1 - axis_at))
    return factor_of


def noise(own_key, dims, deviation, most, cuts=(), held_as=jnp.bfloat16):
    entries = deviation * jax.random.normal(own_key, dims, jnp.float32)
    if cuts:
        entries = entries * block_scale(own_key, dims, cuts, -0.22, 0.18)
    return jnp.clip(entries, -most, most).astype(held_as)


def gaussian_with(own_key, shape, scale, bound, split, heavy, held_as=jnp.bfloat16):
    array = scale * jax.random.normal(own_key, shape, jnp.float32)
    if split:
        array = array * block_scale(own_key, shape, split, -0.22, 0.18)
    return jnp.clip(with_spikes(array, jax.random.fold_in(own_key, 3), *heavy), -bound, bound).astype(held_as)


def setup_inputs(seed: int = 0) -> dict:
    streams_of = jax.random.split(jax.random.key(seed), 9)
    tokens = noise(streams_of[0], (TOKENS, D), 1.0, 6.0, ((0, 32),))
    gain_attn = jnp.clip(1.0 + 0.1 * jax.random.normal(streams_of[1], (D,), jnp.float32), 0.5, 1.5).astype(jnp.bfloat16)
    gain_mlp = jnp.clip(1.0 + 0.1 * jax.random.normal(streams_of[2], (D,), jnp.float32), 0.5, 1.5).astype(jnp.bfloat16)
    w_qkv = noise(streams_of[3], (3, D, D), (D // 2) ** -0.5, 0.3125, ((1, 8), (2, 4)))
    w_out = noise(streams_of[4], (D, D), (D // 16) ** -0.5, 0.875, ((0, 4), (1, 8)))
    w_in = noise(streams_of[5], (2, D, FF), D ** -0.5, 0.21875, ((1, 8), (2, 4)))
    w_down = noise(streams_of[6], (FF, D), FF ** -0.5, 0.1875, ((0, 4), (1, 8)))
    cotangent = gaussian_with(streams_of[7], (TOKENS, D), 1.0, 6.0, ((0, 32),), (0, 1, 32, 2.75))
    return dict(tokens=tokens, gain_attn=gain_attn, gain_mlp=gain_mlp, w_qkv=w_qkv, w_out=w_out, w_in=w_in, w_down=w_down, cotangent=cotangent)


@jax.custom_vjp
def low(v):
    return lax.optimization_barrier(v.astype(jnp.bfloat16)).astype(jnp.float32)

@jax.custom_vjp
def low_back(v):
    return v

def low_keep(v):
    return (low(v), None)

def low_pass(kept, grad):
    return (grad,)

def back_keep(v):
    return (v, None)

def back_low(kept, grad):
    return (low(grad),)
low.defvjp(low_keep, low_pass)
low_back.defvjp(back_keep, back_low)
highest = lax.Precision.HIGHEST
epsilon = 1e-05
rope_base = 160000.0

def gelu_exact(inputs):
    return 0.5 * inputs * (1.0 + jax.scipy.special.erf(inputs * 0.7071067811865476))

def norm_rows(inputs, gain):
    centred = inputs - lax.optimization_barrier(jnp.mean(inputs, axis=-1, keepdims=True))
    spread = lax.optimization_barrier(jnp.mean(centred * centred, axis=-1, keepdims=True))
    return centred * lax.rsqrt(spread + epsilon) * gain

def rotary(length):
    half_size = HEAD // 2
    frequency = rope_base ** (-2.0 * jnp.arange(half_size, dtype=jnp.float32) / HEAD)
    angles = jnp.arange(length, dtype=jnp.float32)[:, None] * frequency[None, :]
    return (jnp.cos(angles)[:, None, :], jnp.sin(angles)[:, None, :])

def rotate(inputs, cosine, sine_table):
    half_size = inputs.shape[-1] // 2
    first_half = inputs[..., :half_size]
    second = inputs[..., half_size:]
    return jnp.concatenate([first_half * cosine - second * sine_table, second * cosine + first_half * sine_table], axis=-1)

def block_layer(inputs, gain_attn, gain_mlp, w_qkv, w_out, w_in, w_down):
    length = inputs.shape[0]
    cosine, sine_table = rotary(length)
    normed_attn = low(norm_rows(inputs, gain_attn))
    projected = low_back(jnp.einsum('td,cde->cte', normed_attn, w_qkv, precision=highest))
    shaped = projected.reshape(3, length, HEADS, HEAD)
    queries = low(rotate(shaped[0], cosine, sine_table))
    keys_rot = low(rotate(shaped[1], cosine, sine_table))
    values = low(shaped[2])
    scores = low_back(jnp.einsum('qhd,khd->hqk', queries, keys_rot, precision=highest) * HEAD ** (-0.5))
    row_max = lax.optimization_barrier(jnp.max(scores, axis=-1, keepdims=True))
    weights = jnp.exp(scores - row_max)
    prob_block = low(weights / lax.optimization_barrier(jnp.sum(weights, axis=-1, keepdims=True)))
    attended = jnp.einsum('hqk,khd->qhd', prob_block, values, precision=highest).reshape(length, HEADS * HEAD)
    attended = low(low_back(attended))
    mixed_attn = inputs + low_back(jnp.dot(attended, w_out, precision=highest))
    normed_mlp = low(norm_rows(mixed_attn, gain_mlp))
    gate_up = low_back(jnp.einsum('td,cdf->ctf', normed_mlp, w_in, precision=highest))
    hidden = low(gelu_exact(gate_up[0]) * gate_up[1])
    return mixed_attn + low_back(jnp.dot(hidden, w_down, precision=highest))

def reference(tokens, gain_attn, gain_mlp, w_qkv, w_out, w_in, w_down, cotangent):
    params = tuple((weight_array.astype(jnp.float32) for weight_array in (gain_attn, gain_mlp, w_qkv, w_out, w_in, w_down)))
    token_rows = tokens.astype(jnp.float32).reshape(TOKENS // LEN, LEN, D)
    cot_rows = cotangent.astype(jnp.float32).reshape(TOKENS // LEN, LEN, D)
    zero_grads = tuple((jnp.zeros_like(weight_array) for weight_array in params))

    def scan_step(grad_total, row_pair):
        layer_out, pullback = jax.vjp(block_layer, row_pair[0], params[0], params[1], params[2], params[3], params[4], params[5])
        gradients = pullback(row_pair[1])
        grad_total = jax.tree.map(jnp.add, grad_total, tuple(gradients[1:]))
        return (grad_total, (layer_out, gradients[0]))
    grad_total, (outputs, input_grads) = lax.scan(scan_step, zero_grads, (token_rows, cot_rows))
    return (outputs.reshape(TOKENS, D).astype(jnp.bfloat16), input_grads.reshape(TOKENS, D), grad_total[0], grad_total[1], grad_total[2], grad_total[3], grad_total[4], grad_total[5])
```

```python
import functools

import jax
import jax.numpy as jnp
from jax import lax
from jax.experimental import pallas as pl
from jax.experimental.pallas import tpu as pltpu
from jax.sharding import PartitionSpec as P

HEAD = 64
LEN = 1024


epsilon = 1e-05
rope_base = 160000.0


def cut_along(array, dim, length):
    dims = array.shape
    pieces = array.reshape(*dims[:dim], length, dims[dim] // length, *dims[dim + 1 :])
    return jnp.moveaxis(pieces, dim, 0)


def summed_on_arrival(array, axis, dim):
    pieces = cut_along(array, dim, lax.axis_size(axis))
    arrived = lax.all_to_all(pieces, axis, split_axis=0, concat_axis=0, tiled=True)
    return arrived.astype(jnp.float32).sum(axis=0)


def gelu_exact(inputs):
    return 0.5 * inputs * (1.0 + jax.scipy.special.erf(inputs * 0.7071067811865476))


def glu_mix(gate_up):
    return gelu_exact(gate_up[0]) * gate_up[1]


def norm_rows(inputs, gain):
    centred = inputs - jnp.mean(inputs, axis=-1, keepdims=True)
    spread = jnp.mean(centred * centred, axis=-1, keepdims=True)
    return centred * lax.rsqrt(spread + epsilon) * gain


def rotary(length):
    half_size = HEAD // 2
    frequency = rope_base ** (-2.0 * jnp.arange(half_size, dtype=jnp.float32) / HEAD)
    angles = jnp.arange(length, dtype=jnp.float32)[:, None] * frequency[None, :]
    return (jnp.cos(angles)[:, None, :], jnp.sin(angles)[:, None, :])


def rotate(inputs, cosine, sine_table):
    half_size = inputs.shape[-1] // 2
    first_half = inputs[..., :half_size]
    second = inputs[..., half_size:]
    return jnp.concatenate(
        [first_half * cosine - second * sine_table, second * cosine + first_half * sine_table],
        axis=-1,
    )


def rotate_back(inputs, cosine, sine_table):
    half_size = inputs.shape[-1] // 2
    first_half = inputs[..., :half_size]
    second = inputs[..., half_size:]
    return jnp.concatenate(
        [first_half * cosine + second * sine_table, second * cosine - first_half * sine_table],
        axis=-1,
    )


def plain_layer(tokens, gain_attn, gain_mlp, w_qkv, w_out, w_in, w_down, cotangent):
    row_count = tokens.shape[0]
    group_rows = row_count * lax.axis_size("tensor")
    seq_count = group_rows // LEN
    block_rows = min(512, LEN)
    block_count = LEN // block_rows
    score_scale = HEAD ** (-0.5)
    inputs = tokens.astype(jnp.float32)
    gain_one, gain_two, qkv_weight, out_weight, in_weight, down_weight = (
        lax.all_gather(gain_attn, "dp", axis=0, tiled=True),
        lax.all_gather(gain_mlp, "dp", axis=0, tiled=True),
        lax.all_gather(w_qkv, "dp", axis=1, tiled=True),
        lax.all_gather(w_out, "dp", axis=1, tiled=True),
        lax.all_gather(w_in, "dp", axis=1, tiled=True),
        lax.all_gather(w_down, "dp", axis=1, tiled=True),
    )
    local_width = qkv_weight.shape[2]
    local_heads = local_width // HEAD
    cosine, sine_table = rotary(LEN)

    def split_blocks(array):
        return array.reshape(seq_count, block_count, block_rows, local_heads, HEAD).transpose(
            1, 0, 2, 3, 4
        )

    def join_blocks(array):
        return array.transpose(1, 0, 2, 3, 4).reshape(seq_count, LEN, local_heads, HEAD)

    normed_attn = norm_rows(inputs, gain_one.astype(jnp.float32)).astype(jnp.bfloat16)
    attn_rows = lax.all_gather(normed_attn, "tensor", axis=0, tiled=True)
    projected = jnp.einsum("td,cde->cte", attn_rows, qkv_weight, preferred_element_type=jnp.float32)
    shaped = projected.reshape(3, seq_count, LEN, local_heads, HEAD)
    queries = rotate(shaped[0], cosine, sine_table).astype(jnp.bfloat16)
    keys_rot = rotate(shaped[1], cosine, sine_table).astype(jnp.bfloat16)
    values = shaped[2].astype(jnp.bfloat16)

    def attend(query_block):
        scores = (
            jnp.einsum("sqhd,skhd->shqk", query_block, keys_rot, preferred_element_type=jnp.float32)
            * score_scale
        )
        row_max = jnp.max(scores, axis=-1, keepdims=True)
        weights = jnp.exp(scores - row_max)
        row_total = jnp.sum(weights, axis=-1, keepdims=True)
        prob_block = (weights / row_total).astype(jnp.bfloat16)
        result = jnp.einsum(
            "shqk,skhd->sqhd", prob_block, values, preferred_element_type=jnp.float32
        )
        return (result.astype(jnp.bfloat16), (row_max + jnp.log(row_total))[..., 0])

    query_blocks = split_blocks(queries)
    attn_blocks, log_totals = lax.map(attend, query_blocks)
    attended = join_blocks(attn_blocks).reshape(group_rows, local_width)
    mixed_attn = inputs + lax.psum_scatter(
        jnp.dot(attended, out_weight, preferred_element_type=jnp.float32),
        "tensor",
        scatter_dimension=0,
        tiled=True,
    )
    normed_mlp = norm_rows(mixed_attn, gain_two.astype(jnp.float32)).astype(jnp.bfloat16)
    mlp_rows = lax.all_gather(normed_mlp, "tensor", axis=0, tiled=True)
    gate_up = jnp.einsum("td,cdf->ctf", mlp_rows, in_weight, preferred_element_type=jnp.float32)
    hidden = glu_mix(gate_up).astype(jnp.bfloat16)
    output = mixed_attn + lax.psum_scatter(
        jnp.dot(hidden, down_weight, preferred_element_type=jnp.float32).astype(jnp.bfloat16),
        "tensor",
        scatter_dimension=0,
        tiled=True,
    ).astype(jnp.float32)
    mixed_out = output.astype(jnp.bfloat16)
    grad_out_rows = lax.all_gather(cotangent, "tensor", axis=0, tiled=True)
    grad_down = jnp.einsum("tf,td->fd", hidden, grad_out_rows, preferred_element_type=jnp.float32)
    grad_hidden = jnp.einsum(
        "td,fd->tf", grad_out_rows, down_weight, preferred_element_type=jnp.float32
    )
    unused_glu, glu_pull = jax.vjp(glu_mix, gate_up)
    grad_gate_up = glu_pull(grad_hidden)[0].astype(jnp.bfloat16)
    grad_in = jnp.einsum("td,ctf->cdf", mlp_rows, grad_gate_up, preferred_element_type=jnp.float32)
    grad_normed_mlp = lax.psum_scatter(
        jnp.einsum(
            "ctf,cdf->td", grad_gate_up, in_weight, preferred_element_type=jnp.float32
        ).astype(jnp.bfloat16),
        "tensor",
        scatter_dimension=0,
        tiled=True,
    ).astype(jnp.float32)
    unused_mlp, norm_pull_mlp = jax.vjp(norm_rows, mixed_attn, gain_two.astype(jnp.float32))
    grad_mixed_part, grad_gain_two = norm_pull_mlp(grad_normed_mlp)
    grad_mixed = cotangent.astype(jnp.float32) + grad_mixed_part
    grad_branch = grad_mixed.astype(jnp.bfloat16)
    branch_rows = lax.all_gather(grad_branch, "tensor", axis=0, tiled=True)
    grad_out_weight = jnp.einsum(
        "te,td->ed", attended, branch_rows, preferred_element_type=jnp.float32
    )
    grad_attended = jnp.einsum(
        "td,ed->te", branch_rows, out_weight, preferred_element_type=jnp.float32
    ).astype(jnp.bfloat16)

    def attend_back(state_pair, block_items):
        grad_keys, grad_values = state_pair
        query_block, grad_block, log_block = block_items
        scores = (
            jnp.einsum("sqhd,skhd->shqk", query_block, keys_rot, preferred_element_type=jnp.float32)
            * score_scale
        )
        prob_block = jnp.exp(scores - log_block[..., None])
        grad_probs = jnp.einsum(
            "sqhd,skhd->shqk", grad_block, values, preferred_element_type=jnp.float32
        )
        inner_sum = jnp.sum(prob_block * grad_probs, axis=-1, keepdims=True)
        grad_scores = (prob_block * (grad_probs - inner_sum)).astype(jnp.bfloat16)
        grad_query = (
            jnp.einsum("shqk,skhd->sqhd", grad_scores, keys_rot, preferred_element_type=jnp.float32)
            * score_scale
        )
        grad_keys = (
            grad_keys
            + jnp.einsum(
                "shqk,sqhd->skhd", grad_scores, query_block, preferred_element_type=jnp.float32
            )
            * score_scale
        )
        grad_values = grad_values + jnp.einsum(
            "shqk,sqhd->skhd",
            prob_block.astype(jnp.bfloat16),
            grad_block,
            preferred_element_type=jnp.float32,
        )
        return ((grad_keys, grad_values), grad_query)

    zero_state = jnp.zeros((seq_count, LEN, local_heads, HEAD), jnp.float32)
    (grad_keys, grad_values), grad_queries = lax.scan(
        attend_back,
        (zero_state, zero_state),
        (query_blocks, split_blocks(grad_attended), log_totals),
    )
    grad_projected = (
        jnp.stack(
            [
                rotate_back(join_blocks(grad_queries), cosine, sine_table),
                rotate_back(grad_keys, cosine, sine_table),
                grad_values,
            ]
        )
        .reshape(3, group_rows, local_width)
        .astype(jnp.bfloat16)
    )
    grad_qkv = jnp.einsum(
        "td,cte->cde", attn_rows, grad_projected, preferred_element_type=jnp.float32
    )
    grad_normed_attn = lax.psum_scatter(
        jnp.einsum(
            "cte,cde->td", grad_projected, qkv_weight, preferred_element_type=jnp.float32
        ).astype(jnp.bfloat16),
        "tensor",
        scatter_dimension=0,
        tiled=True,
    ).astype(jnp.float32)
    unused_attn, norm_pull_attn = jax.vjp(norm_rows, inputs, gain_one.astype(jnp.float32))
    grad_inputs_part, grad_gain_one = norm_pull_attn(grad_normed_attn)
    input_grad = grad_mixed + grad_inputs_part
    gain_sums = lax.psum(jnp.stack([grad_gain_one, grad_gain_two]), "tensor")
    gain_part, qkv_part, out_part, in_part, down_part = (
        summed_on_arrival(gain_sums.astype(jnp.bfloat16), "dp", 1),
        summed_on_arrival(grad_qkv.astype(jnp.bfloat16), "dp", 1),
        summed_on_arrival(grad_out_weight.astype(jnp.bfloat16), "dp", 1),
        summed_on_arrival(grad_in.astype(jnp.bfloat16), "dp", 1),
        summed_on_arrival(grad_down.astype(jnp.bfloat16), "dp", 1),
    )
    return (
        mixed_out,
        input_grad,
        gain_part[0],
        gain_part[1],
        qkv_part,
        out_part,
        in_part,
        down_part,
    )


bf16 = jnp.bfloat16
f32 = jnp.float32


def mm(a, b):
    return lax.dot_general(a, b, (((1,), (0,)), ((), ())), preferred_element_type=f32)


def mm_nt(a, b):
    return lax.dot_general(a, b, (((1,), (1,)), ((), ())), preferred_element_type=f32)


def mm_tn(a, b):
    return lax.dot_general(a, b, (((0,), (0,)), ((), ())), preferred_element_type=f32)


def layer_kernel(
    dp, rows, width, ff, ffp,
    tokens, gain_a, gain_m, w_qkv, w_out, w_in, w_down, cotangent, cos_t, sin_t,
    mixed, input_grad, gga_out, ggm_out, gqkv_out, gout_out, gin_out, gdown_out,
    gpk, gbuf, pa, pb, nbuf, cbuf, mbuf, bbuf,
    wgu, wdt, wot,
    qs, qt, km, vm, probs, att, gatt, gproj, gqs, gkt, gvt,
    hid, ggu,
    xh1, xh2, res, gmix, keep,
    s1, r1, s2, r2,
    ga_s, ga_r, go_s, go_r, gb_s, gb_r, gt, gd_s, gd_r,
    ss, rs,
):
    me = lax.axis_index("dp")
    t = lax.axis_index("tensor")
    x = lax.div(t, 2)
    c = lax.rem(t, 2)
    partner = x * 2 + (1 - c)
    cross = (1 - x) * 2 + c
    diag = (1 - x) * 2 + (1 - c)
    shard = w_qkv.shape[1]
    model = tokens.shape[1]
    group = 4 * rows
    counter = [0]
    sent = []

    def slot():
        counter[0] += 1
        return counter[0] - 1

    def remote(source, target, k, d, tn):
        return pltpu.make_async_remote_copy(
            src_ref=source, dst_ref=target, send_sem=ss.at[k], recv_sem=rs.at[k],
            device_id=(d, tn), device_id_type=pl.DeviceIdType.MESH,
        )

    def send(source, target, k, d, tn):
        copy = remote(source, target, k, d, tn)
        copy.start()
        sent.append(copy)

    barrier = pltpu.get_barrier_semaphore()
    for i in range(1, dp):
        pl.semaphore_signal(barrier, inc=1, device_id=(lax.rem(me + i, dp), t),
                            device_id_type=pl.DeviceIdType.MESH)
    for other in (partner, cross, diag):
        pl.semaphore_signal(barrier, inc=1, device_id=(me, other),
                            device_id_type=pl.DeviceIdType.MESH)

    gpk[...] = jnp.zeros_like(gpk)
    gpk[0:1, 0:shard] = gain_a[...].astype(f32)
    gpk[1:2, 0:shard] = gain_m[...].astype(f32)
    gbuf[me] = gpk[...]
    own = [w_qkv[i] for i in range(3)] + [w_out[...].astype(f32).T.astype(bf16)]
    pa[me] = jnp.concatenate(own, axis=1)
    blank = jnp.zeros((shard, ffp - ff), bf16)
    pb[me] = jnp.concatenate(
        [w_in[0], blank, w_in[1], blank, w_down[...].astype(f32).T.astype(bf16), blank], axis=1)
    cbuf[t] = cotangent[...]

    pl.semaphore_wait(barrier, dp - 1 + 3)

    def gather_dp(buf):
        slots = []
        for i in range(1, dp):
            k = slot()
            slots.append(k)
            send(buf.at[me], buf.at[me], k, lax.rem(me + i, dp), t)
        return slots

    def gather_dp_wait(buf, slots):
        for i in range(1, dp):
            origin = lax.rem(me + dp - i, dp)
            remote(buf.at[origin], buf.at[origin], slots[i - 1], origin, t).wait_recv()

    def rows_start(buf):
        slots = [slot(), slot(), slot()]
        send(buf.at[t], buf.at[t], slots[1], me, cross)
        send(buf.at[t], buf.at[t], slots[0], me, partner)
        return slots

    def rows_partner(buf, slots):
        remote(buf.at[partner], buf.at[partner], slots[0], me, partner).wait_recv()

    def rows_cross(buf, slots):
        remote(buf.at[cross], buf.at[cross], slots[1], me, cross).wait_recv()
        send(buf.at[cross], buf.at[cross], slots[2], me, partner)

    def rows_diag(buf, slots):
        remote(buf.at[diag], buf.at[diag], slots[2], me, partner).wait_recv()

    def sum_init(n):
        return (n, [slot(), slot(), slot()])

    def sum_diag(state, value):
        n, k = state
        s1[n, 0] = value.astype(bf16)
        send(s1.at[n, 0], r1.at[n, 0], k[0], me, partner)

    def sum_partner(state, value):
        n, k = state
        s1[n, 1] = value.astype(bf16)
        send(s1.at[n, 1], r1.at[n, 1], k[1], me, partner)

    def sum_cross(state, value):
        n, k = state
        remote(s1.at[n, 0], r1.at[n, 0], k[0], me, partner).wait_recv()
        s2[n] = (value + r1[n, 0].astype(f32)).astype(bf16)
        send(s2.at[n], r2.at[n], k[2], me, cross)

    def sum_own(state):
        n, k = state
        remote(s1.at[n, 1], r1.at[n, 1], k[1], me, partner).wait_recv()
        remote(s2.at[n], r2.at[n], k[2], me, cross).wait_recv()
        return r1[n, 1].astype(f32) + r2[n].astype(f32)

    def norm_parts(value):
        centred = value - jnp.mean(value, axis=-1, keepdims=True)
        spread = jnp.mean(centred * centred, axis=-1, keepdims=True)
        inverse = lax.rsqrt(spread + epsilon)
        return centred * inverse, inverse

    def norm_back(grad, gain, unit, inverse):
        scaled = grad * gain
        first = jnp.mean(scaled, axis=-1, keepdims=True)
        second = jnp.mean(scaled * unit, axis=-1, keepdims=True)
        return (inverse * (scaled - first - unit * second),
                jnp.sum(grad * unit, axis=0, keepdims=True))

    lanes = lax.broadcasted_iota(jnp.int32, (rows, 2 * width), 1)
    low_half = lax.rem(lanes, HEAD) < HEAD // 2

    def turn(value, b, sign):
        other = jnp.where(low_half, pltpu.roll(value, 2 * width - HEAD // 2, 1),
                          pltpu.roll(value, HEAD // 2, 1))
        times = 2 * width // 128
        cosine = jnp.concatenate([cos_t[b]] * times, axis=1)
        sine = jnp.concatenate([sin_t[b]] * times, axis=1)
        return value * cosine + sign * (other * sine)

    heads = width // HEAD
    scale = HEAD ** -0.5

    gain_slots = gather_dp(gbuf)
    pa_slots = gather_dp(pa)
    unit, inverse1 = norm_parts(tokens[...].astype(f32))
    xh1[...] = unit
    gather_dp_wait(gbuf, gain_slots)
    gain1 = jnp.concatenate([gbuf[j, 0:1, 0:shard] for j in range(dp)], axis=1)
    gain2 = jnp.concatenate([gbuf[j, 1:2, 0:shard] for j in range(dp)], axis=1)
    nbuf[t] = (unit * gain1).astype(bf16)
    n_slots = rows_start(nbuf)
    c_slots = rows_start(cbuf)
    gather_dp_wait(pa, pa_slots)
    pb_slots = gather_dp(pb)
    wot[...] = pa[...].reshape(model, 4 * width)[:, 3 * width:]
    head_of = lax.div(lax.broadcasted_iota(jnp.int32, (rows, width), 1), HEAD)

    def project(b):
        proj = mm(nbuf[b], pa[...].reshape(model, 4 * width)[:, : 3 * width])
        turned = turn(proj[:, : 2 * width], b, 1.0)
        q = turned[:, :width]
        kk = turned[:, width:]
        vv = proj[:, 2 * width:]
        qs[b] = q.astype(bf16)
        qt[b] = q.T.astype(bf16)
        place = pl.ds(pl.multiple_of(b * rows, rows), rows)
        for h in range(heads):
            km[h, place, :] = jnp.where(head_of == h, kk, 0.0).astype(bf16)
            vm[h, place, :] = jnp.where(head_of == h, vv, 0.0).astype(bf16)

    project(t)
    rows_partner(nbuf, n_slots)
    project(partner)
    rows_cross(nbuf, n_slots)
    project(cross)
    rows_diag(nbuf, n_slots)
    project(diag)

    def attend(i, carry):
        q = qs[i]
        acc = jnp.zeros((rows, width), f32)
        for h in range(heads):
            s = mm_nt(q, km[h]) * scale
            e = jnp.exp(s - jnp.max(s, axis=-1, keepdims=True))
            p = e * (1.0 / jnp.sum(e, axis=-1, keepdims=True))
            probs[h, i] = p
            acc = acc + mm(p.astype(bf16), vm[h])
        att[i] = acc.astype(bf16)
        return carry

    lax.fori_loop(0, 4, attend, 0)

    st = sum_init(0)
    sum_diag(st, mm_nt(att[diag], wot[...]))
    sum_partner(st, mm_nt(att[partner], wot[...]))
    sum_cross(st, mm_nt(att[cross], wot[...]))
    keep[0] = mm_nt(att[t], wot[...])
    rows_cross(cbuf, c_slots)
    rows_partner(cbuf, c_slots)
    rows_diag(cbuf, c_slots)
    gather_dp_wait(pb, pb_slots)
    everything = pb[...].reshape(model, 3 * ffp)
    wgu[...] = everything[:, : 2 * ffp]
    wdt[...] = everything[:, 2 * ffp:]
    res[...] = tokens[...].astype(f32) + (keep[0] + sum_own(st))
    unit2, inverse2 = norm_parts(res[...])
    xh2[...] = unit2
    mbuf[t] = (unit2 * gain2).astype(bf16)
    m_slots = rows_start(mbuf)

    def mlp(b):
        gu = mm(mbuf[b], wgu[...])
        gate = gu[:, :ffp]
        up = gu[:, ffp:]
        phi = 0.5 * (1.0 + lax.erf(gate * 0.7071067811865476))
        act = gate * phi
        hid[b] = (act * up).astype(bf16)
        gh = mm(cbuf[b], wdt[...])
        slope = phi + gate * (jnp.exp(-0.5 * gate * gate) * 0.3989422804014327)
        ggu[b, :, :ffp] = (gh * up * slope).astype(bf16)
        ggu[b, :, ffp:] = (gh * act).astype(bf16)

    st_g = sum_init(1)
    mlp(t)
    keep[0] = mm_nt(ggu[t], wgu[...])
    rows_partner(mbuf, m_slots)
    mlp(partner)
    sum_partner(st_g, mm_nt(ggu[partner], wgu[...]))
    rows_cross(mbuf, m_slots)
    rows_diag(mbuf, m_slots)
    mlp(diag)
    sum_diag(st_g, mm_nt(ggu[diag], wgu[...]))
    mlp(cross)
    sum_cross(st_g, mm_nt(ggu[cross], wgu[...]))

    mflat = mbuf[...].reshape(group, model)

    def reduce_dp(buf, received):
        slots = []
        for i in range(1, dp):
            k = slot()
            slots.append(k)
            peer = lax.rem(me + i, dp)
            send(buf.at[peer], received.at[me], k, peer, t)
        return slots

    def reduce_dp_wait(buf, received, slots):
        total = buf[me].astype(f32)
        for i in range(1, dp):
            origin = lax.rem(me + dp - i, dp)
            remote(buf.at[origin], received.at[origin], slots[i - 1], origin, t).wait_recv()
            total = total + received[origin].astype(f32)
        return total

    for part in range(2):
        cut = slice(part * ffp, (part + 1) * ffp)
        piece = mm_tn(mflat, ggu[:, :, cut].reshape(group, ffp))
        gb_s[:, :, cut] = piece.astype(bf16).reshape(dp, shard, ffp)

    gnm = keep[0] + sum_own(st_g)
    back2, ggm = norm_back(gnm, gain2, xh2[...], inverse2)
    gmix[...] = cotangent[...].astype(f32) + back2
    bbuf[t] = gmix[...].astype(bf16)
    b_slots = rows_start(bbuf)

    st_d = sum_init(2)
    sum_diag(st_d, mm_nt(hid[diag], wdt[...]))
    sum_partner(st_d, mm_nt(hid[partner], wdt[...]))
    piece = mm_tn(cbuf[...].reshape(group, model), hid[...].reshape(group, ffp))
    gb_s[:, :, 2 * ffp:] = piece.astype(bf16).reshape(dp, shard, ffp)
    gb_slots = reduce_dp(gb_s, gb_r)
    rows_cross(bbuf, b_slots)
    sum_cross(st_d, mm_nt(hid[cross], wdt[...]))
    keep[0] = mm_nt(hid[t], wdt[...])
    rows_partner(bbuf, b_slots)
    rows_diag(bbuf, b_slots)

    gkt[...] = jnp.zeros_like(gkt)
    gvt[...] = jnp.zeros_like(gvt)

    def attend_back(i, carry):
        ga = mm(bbuf[i], wot[...])
        gab = ga.astype(bf16)
        gatt[i] = gab
        gat = ga.T.astype(bf16)
        acc = jnp.zeros((rows, width), f32)
        for h in range(heads):
            some = slice(h * HEAD, (h + 1) * HEAD)
            gp = mm_nt(gab, vm[h])
            p = probs[h, i]
            inner = jnp.sum(p * gp, axis=-1, keepdims=True)
            gs = (p * (gp - inner)).astype(bf16)
            acc = acc + mm(gs, km[h])
            gkt[some, :] += mm(qt[i, some, :], gs)
            gvt[some, :] += mm(gat[some, :], p.astype(bf16))
        gqs[i] = acc * scale
        return carry

    lax.fori_loop(0, 4, attend_back, 0)

    piece = mm_tn(bbuf[...].reshape(group, model), att[...].reshape(group, width))
    go_s[...] = piece.astype(bf16).reshape(dp, shard, width)
    go_slots = reduce_dp(go_s, go_r)

    def join(b, carry):
        place = pl.ds(pl.multiple_of(b * rows, rows), rows)
        gk = gkt[:, place].T * scale
        back = turn(jnp.concatenate([gqs[b], gk], axis=1), b, -1.0)
        gproj[b, :, : 2 * width] = back.astype(bf16)
        gproj[b, :, 2 * width:] = gvt[:, place].T.astype(bf16)
        return carry

    lax.fori_loop(0, 4, join, 0)
    wqkv = pa[...].reshape(model, 4 * width)[:, : 3 * width]
    mixed[...] = (res[...] + (keep[0] + sum_own(st_d))).astype(bf16)
    st_a = sum_init(3)
    sum_diag(st_a, mm_nt(gproj[diag], wqkv))
    sum_partner(st_a, mm_nt(gproj[partner], wqkv))
    sum_cross(st_a, mm_nt(gproj[cross], wqkv))
    piece = mm_tn(nbuf[...].reshape(group, model), gproj[...].reshape(group, 3 * width))
    ga_s[...] = piece.astype(bf16).reshape(dp, shard, 3 * width)
    ga_slots = reduce_dp(ga_s, ga_r)
    keep[0] = mm_nt(gproj[t], wqkv)

    total = reduce_dp_wait(gb_s, gb_r, gb_slots)
    gin_out[0] = total[:, :ff]
    gin_out[1] = total[:, ffp: ffp + ff]
    gdown_out[...] = total[:, 2 * ffp:].T[:ff]
    total = reduce_dp_wait(go_s, go_r, go_slots)
    gout_out[...] = total.T

    gna = keep[0] + sum_own(st_a)
    back1, gga = norm_back(gna, gain1, xh1[...], inverse1)
    gt[t] = jnp.concatenate([gga, ggm, jnp.zeros((6, model), f32)], axis=0)
    tslots = [slot(), slot(), slot()]
    for k, other in zip(tslots, (partner, cross, diag)):
        send(gt.at[t], gt.at[t], k, me, other)
    input_grad[...] = gmix[...] + back1
    for k, other in zip(tslots, (partner, cross, diag)):
        remote(gt.at[other], gt.at[other], k, me, other).wait_recv()
    gains = (gt[0] + gt[1]) + (gt[2] + gt[3])
    for j in range(dp):
        gd_s[j, :, 0:shard] = gains[:, j * shard:(j + 1) * shard]
        gd_s[j, :, shard:] = jnp.zeros((8, 128 - shard), f32)
    gd_slots = reduce_dp(gd_s, gd_r)
    total = reduce_dp_wait(ga_s, ga_r, ga_slots)
    for i in range(3):
        gqkv_out[i] = total[:, i * width:(i + 1) * width]
    total = reduce_dp_wait(gd_s, gd_r, gd_slots)
    gga_out[...] = total[0:1, :shard]
    ggm_out[...] = total[1:2, :shard]
    for copy in sent:
        copy.wait_send()


def per_device(tokens, gain_attn, gain_mlp, w_qkv, w_out, w_in, w_down, cotangent):
    dp = lax.axis_size("dp")
    rows, model = tokens.shape
    shard, width = w_qkv.shape[1:]
    ff = w_in.shape[2]
    one_sequence = lax.axis_size("tensor") == 4 and rows * 4 == LEN
    if not (one_sequence and shard % 16 == 0 and shard <= 128 and 2 * width % 128 == 0):
        return plain_layer(tokens, gain_attn, gain_mlp, w_qkv, w_out, w_in, w_down, cotangent)
    ffp = -(-ff // 128) * 128
    cosine, sine = rotary(LEN)
    cosine, sine = cosine[:, 0], sine[:, 0]
    cos_t = jnp.concatenate([cosine] * 4, axis=1).reshape(4, rows, 2 * HEAD)
    sin_t = jnp.concatenate([-sine, sine] * 2, axis=1).reshape(4, rows, 2 * HEAD)
    vmem = pltpu.VMEM
    scratch = [
        vmem((8, 128), f32), vmem((dp, 8, 128), f32),
        vmem((dp, shard, 4 * width), bf16), vmem((dp, shard, 3 * ffp), bf16),
        vmem((4, rows, model), bf16), vmem((4, rows, model), bf16),
        vmem((4, rows, model), bf16), vmem((4, rows, model), bf16),
        vmem((model, 2 * ffp), bf16), vmem((model, ffp), bf16), vmem((model, width), bf16),
        vmem((4, rows, width), bf16), vmem((4, width, rows), bf16),
        vmem((width // HEAD, LEN, width), bf16), vmem((width // HEAD, LEN, width), bf16),
        vmem((width // HEAD, 4, rows, LEN), f32),
        vmem((4, rows, width), bf16), vmem((4, rows, width), bf16),
        vmem((4, rows, 3 * width), bf16), vmem((4, rows, width), f32),
        vmem((width, LEN), f32), vmem((width, LEN), f32),
        vmem((4, rows, ffp), bf16), vmem((4, rows, 2 * ffp), bf16),
        vmem((rows, model), f32), vmem((rows, model), f32),
        vmem((rows, model), f32), vmem((rows, model), f32), vmem((1, rows, model), f32),
        vmem((4, 2, rows, model), bf16), vmem((4, 2, rows, model), bf16),
        vmem((4, rows, model), bf16), vmem((4, rows, model), bf16),
        vmem((dp, shard, 3 * width), bf16), vmem((dp, shard, 3 * width), bf16),
        vmem((dp, shard, width), bf16), vmem((dp, shard, width), bf16),
        vmem((dp, shard, 3 * ffp), bf16), vmem((dp, shard, 3 * ffp), bf16),
        vmem((4, 8, model), f32), vmem((dp, 8, 128), f32), vmem((dp, 8, 128), f32),
        pltpu.SemaphoreType.DMA((7 * (dp - 1) + 27,)),
        pltpu.SemaphoreType.DMA((7 * (dp - 1) + 27,)),
    ]
    whole = pl.BlockSpec(memory_space=pltpu.VMEM)
    shape = jax.ShapeDtypeStruct
    outs = pl.pallas_call(
        functools.partial(layer_kernel, dp, rows, width, ff, ffp),
        out_shape=[
            shape((rows, model), bf16), shape((rows, model), f32),
            shape((1, shard), f32), shape((1, shard), f32),
            shape(w_qkv.shape, f32), shape(w_out.shape, f32),
            shape(w_in.shape, f32), shape(w_down.shape, f32),
        ],
        in_specs=[whole] * 10,
        out_specs=[whole] * 8,
        scratch_shapes=scratch,
        compiler_params=pltpu.CompilerParams(
            collective_id=0, has_side_effects=True, vmem_limit_bytes=62 * 1024 * 1024),
    )(tokens, gain_attn[None], gain_mlp[None], w_qkv, w_out, w_in, w_down, cotangent, cos_t, sin_t)
    mixed, input_grad, gga, ggm, gqkv, gout, gin, gdown = outs
    return mixed, input_grad, gga[0], ggm[0], gqkv, gout, gin, gdown


def solution(mesh):
    placed = (
        P(("dp", "tensor"), None),
        P("dp"),
        P("dp"),
        P(None, "dp", "tensor"),
        P("tensor", "dp"),
        P(None, "dp", "tensor"),
        P("tensor", "dp"),
        P(("dp", "tensor"), None),
    )
    return jax.shard_map(
        per_device,
        mesh=mesh,
        in_specs=placed,
        out_specs=(
            P(("dp", "tensor"), None),
            P(("dp", "tensor"), None),
            P("dp"),
            P("dp"),
            P(None, "dp", "tensor"),
            P("tensor", "dp"),
            P(None, "dp", "tensor"),
            P("tensor", "dp"),
        ),
        check_vma=False,
    )
```

```python
import functools

import numpy as np
import jax
import jax.numpy as jnp
from jax import lax
from jax.experimental import pallas as pl
from jax.experimental.pallas import tpu as pltpu
from jax.sharding import PartitionSpec as P

HEAD = 64
LEN = 1024


epsilon = 1e-05
rope_base = 160000.0


def cut_along(array, dim, length):
    dims = array.shape
    pieces = array.reshape(*dims[:dim], length, dims[dim] // length, *dims[dim + 1 :])
    return jnp.moveaxis(pieces, dim, 0)


def summed_on_arrival(array, axis, dim):
    pieces = cut_along(array, dim, lax.axis_size(axis))
    arrived = lax.all_to_all(pieces, axis, split_axis=0, concat_axis=0, tiled=True)
    return arrived.astype(jnp.float32).sum(axis=0)


def gelu_exact(inputs):
    return 0.5 * inputs * (1.0 + jax.scipy.special.erf(inputs * 0.7071067811865476))


def glu_mix(gate_up):
    return gelu_exact(gate_up[0]) * gate_up[1]


def norm_rows(inputs, gain):
    centred = inputs - jnp.mean(inputs, axis=-1, keepdims=True)
    spread = jnp.mean(centred * centred, axis=-1, keepdims=True)
    return centred * lax.rsqrt(spread + epsilon) * gain


def rotary(length):
    half_size = HEAD // 2
    frequency = rope_base ** (-2.0 * jnp.arange(half_size, dtype=jnp.float32) / HEAD)
    angles = jnp.arange(length, dtype=jnp.float32)[:, None] * frequency[None, :]
    return (jnp.cos(angles)[:, None, :], jnp.sin(angles)[:, None, :])


def rotate(inputs, cosine, sine_table):
    half_size = inputs.shape[-1] // 2
    first_half = inputs[..., :half_size]
    second = inputs[..., half_size:]
    return jnp.concatenate(
        [first_half * cosine - second * sine_table, second * cosine + first_half * sine_table],
        axis=-1,
    )


def rotate_back(inputs, cosine, sine_table):
    half_size = inputs.shape[-1] // 2
    first_half = inputs[..., :half_size]
    second = inputs[..., half_size:]
    return jnp.concatenate(
        [first_half * cosine + second * sine_table, second * cosine - first_half * sine_table],
        axis=-1,
    )


def plain_layer(tokens, gain_attn, gain_mlp, w_qkv, w_out, w_in, w_down, cotangent):
    row_count = tokens.shape[0]
    group_rows = row_count * lax.axis_size("tensor")
    seq_count = group_rows // LEN
    block_rows = min(512, LEN)
    block_count = LEN // block_rows
    score_scale = HEAD ** (-0.5)
    inputs = tokens.astype(jnp.float32)
    gain_one, gain_two, qkv_weight, out_weight, in_weight, down_weight = (
        lax.all_gather(gain_attn, "dp", axis=0, tiled=True),
        lax.all_gather(gain_mlp, "dp", axis=0, tiled=True),
        lax.all_gather(w_qkv, "dp", axis=1, tiled=True),
        lax.all_gather(w_out, "dp", axis=1, tiled=True),
        lax.all_gather(w_in, "dp", axis=1, tiled=True),
        lax.all_gather(w_down, "dp", axis=1, tiled=True),
    )
    local_width = qkv_weight.shape[2]
    local_heads = local_width // HEAD
    cosine, sine_table = rotary(LEN)

    def split_blocks(array):
        return array.reshape(seq_count, block_count, block_rows, local_heads, HEAD).transpose(
            1, 0, 2, 3, 4
        )

    def join_blocks(array):
        return array.transpose(1, 0, 2, 3, 4).reshape(seq_count, LEN, local_heads, HEAD)

    normed_attn = norm_rows(inputs, gain_one.astype(jnp.float32)).astype(jnp.bfloat16)
    attn_rows = lax.all_gather(normed_attn, "tensor", axis=0, tiled=True)
    projected = jnp.einsum("td,cde->cte", attn_rows, qkv_weight, preferred_element_type=jnp.float32)
    shaped = projected.reshape(3, seq_count, LEN, local_heads, HEAD)
    queries = rotate(shaped[0], cosine, sine_table).astype(jnp.bfloat16)
    keys_rot = rotate(shaped[1], cosine, sine_table).astype(jnp.bfloat16)
    values = shaped[2].astype(jnp.bfloat16)

    def attend(query_block):
        scores = (
            jnp.einsum("sqhd,skhd->shqk", query_block, keys_rot, preferred_element_type=jnp.float32)
            * score_scale
        )
        row_max = jnp.max(scores, axis=-1, keepdims=True)
        weights = jnp.exp(scores - row_max)
        row_total = jnp.sum(weights, axis=-1, keepdims=True)
        prob_block = (weights / row_total).astype(jnp.bfloat16)
        result = jnp.einsum(
            "shqk,skhd->sqhd", prob_block, values, preferred_element_type=jnp.float32
        )
        return (result.astype(jnp.bfloat16), (row_max + jnp.log(row_total))[..., 0])

    query_blocks = split_blocks(queries)
    attn_blocks, log_totals = lax.map(attend, query_blocks)
    attended = join_blocks(attn_blocks).reshape(group_rows, local_width)
    mixed_attn = inputs + lax.psum_scatter(
        jnp.dot(attended, out_weight, preferred_element_type=jnp.float32),
        "tensor",
        scatter_dimension=0,
        tiled=True,
    )
    normed_mlp = norm_rows(mixed_attn, gain_two.astype(jnp.float32)).astype(jnp.bfloat16)
    mlp_rows = lax.all_gather(normed_mlp, "tensor", axis=0, tiled=True)
    gate_up = jnp.einsum("td,cdf->ctf", mlp_rows, in_weight, preferred_element_type=jnp.float32)
    hidden = glu_mix(gate_up).astype(jnp.bfloat16)
    output = mixed_attn + lax.psum_scatter(
        jnp.dot(hidden, down_weight, preferred_element_type=jnp.float32).astype(jnp.bfloat16),
        "tensor",
        scatter_dimension=0,
        tiled=True,
    ).astype(jnp.float32)
    mixed_out = output.astype(jnp.bfloat16)
    grad_out_rows = lax.all_gather(cotangent, "tensor", axis=0, tiled=True)
    grad_down = jnp.einsum("tf,td->fd", hidden, grad_out_rows, preferred_element_type=jnp.float32)
    grad_hidden = jnp.einsum(
        "td,fd->tf", grad_out_rows, down_weight, preferred_element_type=jnp.float32
    )
    unused_glu, glu_pull = jax.vjp(glu_mix, gate_up)
    grad_gate_up = glu_pull(grad_hidden)[0].astype(jnp.bfloat16)
    grad_in = jnp.einsum("td,ctf->cdf", mlp_rows, grad_gate_up, preferred_element_type=jnp.float32)
    grad_normed_mlp = lax.psum_scatter(
        jnp.einsum(
            "ctf,cdf->td", grad_gate_up, in_weight, preferred_element_type=jnp.float32
        ).astype(jnp.bfloat16),
        "tensor",
        scatter_dimension=0,
        tiled=True,
    ).astype(jnp.float32)
    unused_mlp, norm_pull_mlp = jax.vjp(norm_rows, mixed_attn, gain_two.astype(jnp.float32))
    grad_mixed_part, grad_gain_two = norm_pull_mlp(grad_normed_mlp)
    grad_mixed = cotangent.astype(jnp.float32) + grad_mixed_part
    grad_branch = grad_mixed.astype(jnp.bfloat16)
    branch_rows = lax.all_gather(grad_branch, "tensor", axis=0, tiled=True)
    grad_out_weight = jnp.einsum(
        "te,td->ed", attended, branch_rows, preferred_element_type=jnp.float32
    )
    grad_attended = jnp.einsum(
        "td,ed->te", branch_rows, out_weight, preferred_element_type=jnp.float32
    ).astype(jnp.bfloat16)

    def attend_back(state_pair, block_items):
        grad_keys, grad_values = state_pair
        query_block, grad_block, log_block = block_items
        scores = (
            jnp.einsum("sqhd,skhd->shqk", query_block, keys_rot, preferred_element_type=jnp.float32)
            * score_scale
        )
        prob_block = jnp.exp(scores - log_block[..., None])
        grad_probs = jnp.einsum(
            "sqhd,skhd->shqk", grad_block, values, preferred_element_type=jnp.float32
        )
        inner_sum = jnp.sum(prob_block * grad_probs, axis=-1, keepdims=True)
        grad_scores = (prob_block * (grad_probs - inner_sum)).astype(jnp.bfloat16)
        grad_query = (
            jnp.einsum("shqk,skhd->sqhd", grad_scores, keys_rot, preferred_element_type=jnp.float32)
            * score_scale
        )
        grad_keys = (
            grad_keys
            + jnp.einsum(
                "shqk,sqhd->skhd", grad_scores, query_block, preferred_element_type=jnp.float32
            )
            * score_scale
        )
        grad_values = grad_values + jnp.einsum(
            "shqk,sqhd->skhd",
            prob_block.astype(jnp.bfloat16),
            grad_block,
            preferred_element_type=jnp.float32,
        )
        return ((grad_keys, grad_values), grad_query)

    zero_state = jnp.zeros((seq_count, LEN, local_heads, HEAD), jnp.float32)
    (grad_keys, grad_values), grad_queries = lax.scan(
        attend_back,
        (zero_state, zero_state),
        (query_blocks, split_blocks(grad_attended), log_totals),
    )
    grad_projected = (
        jnp.stack(
            [
                rotate_back(join_blocks(grad_queries), cosine, sine_table),
                rotate_back(grad_keys, cosine, sine_table),
                grad_values,
            ]
        )
        .reshape(3, group_rows, local_width)
        .astype(jnp.bfloat16)
    )
    grad_qkv = jnp.einsum(
        "td,cte->cde", attn_rows, grad_projected, preferred_element_type=jnp.float32
    )
    grad_normed_attn = lax.psum_scatter(
        jnp.einsum(
            "cte,cde->td", grad_projected, qkv_weight, preferred_element_type=jnp.float32
        ).astype(jnp.bfloat16),
        "tensor",
        scatter_dimension=0,
        tiled=True,
    ).astype(jnp.float32)
    unused_attn, norm_pull_attn = jax.vjp(norm_rows, inputs, gain_one.astype(jnp.float32))
    grad_inputs_part, grad_gain_one = norm_pull_attn(grad_normed_attn)
    input_grad = grad_mixed + grad_inputs_part
    gain_sums = lax.psum(jnp.stack([grad_gain_one, grad_gain_two]), "tensor")
    gain_part, qkv_part, out_part, in_part, down_part = (
        summed_on_arrival(gain_sums.astype(jnp.bfloat16), "dp", 1),
        summed_on_arrival(grad_qkv.astype(jnp.bfloat16), "dp", 1),
        summed_on_arrival(grad_out_weight.astype(jnp.bfloat16), "dp", 1),
        summed_on_arrival(grad_in.astype(jnp.bfloat16), "dp", 1),
        summed_on_arrival(grad_down.astype(jnp.bfloat16), "dp", 1),
    )
    return (
        mixed_out,
        input_grad,
        gain_part[0],
        gain_part[1],
        qkv_part,
        out_part,
        in_part,
        down_part,
    )


bf16 = jnp.bfloat16
f32 = jnp.float32


def mm(a, b):
    return lax.dot_general(a, b, (((1,), (0,)), ((), ())), preferred_element_type=f32)


def mm_nt(a, b):
    return lax.dot_general(a, b, (((1,), (1,)), ((), ())), preferred_element_type=f32)


def mm_tn(a, b):
    return lax.dot_general(a, b, (((0,), (0,)), ((), ())), preferred_element_type=f32)


def layer_kernel(
    dp, rows, width, ff, ffp,
    tokens, gain_a, gain_m, w_qkv, w_out, w_in, w_down, cotangent, cos_t, sin_t,
    mixed, input_grad, gga_out, ggm_out, gqkv_out, gout_out, gin_out, gdown_out,
    gpk, gbuf, pa, pb, nbuf, cbuf, mbuf, bbuf,
    wgu, wdt, wot,
    qs, qt, km, vm, probs, att, gatt, gproj, gqs, gkt, gvt,
    hid, ggu,
    xh1, xh2, res, gmix, keep,
    s1, r1, s2, r2,
    ga_s, ga_y, ga_z, go_s, go_y, go_z, gb_s, gb_y, gb_z, gf_s, gf_y, gf_z, gt, gd_s, gd_r,
    ss, rs,
):
    me = lax.axis_index("dp")
    t = lax.axis_index("tensor")
    x = lax.div(t, 2)
    c = lax.rem(t, 2)
    partner = x * 2 + (1 - c)
    cross = (1 - x) * 2 + c
    diag = (1 - x) * 2 + (1 - c)
    shard = w_qkv.shape[1]
    model = tokens.shape[1]
    group = 4 * rows
    counter = [0]
    sent = []

    def slot():
        counter[0] += 1
        return counter[0] - 1

    def remote(source, target, k, d, tn):
        return pltpu.make_async_remote_copy(
            src_ref=source, dst_ref=target, send_sem=ss.at[k], recv_sem=rs.at[k],
            device_id=(d, tn), device_id_type=pl.DeviceIdType.MESH,
        )

    def send(source, target, k, d, tn):
        copy = remote(source, target, k, d, tn)
        copy.start()
        sent.append(copy)

    barrier = pltpu.get_barrier_semaphore()
    for i in range(1, dp):
        pl.semaphore_signal(barrier, inc=1, device_id=(lax.rem(me + i, dp), t),
                            device_id_type=pl.DeviceIdType.MESH)
    for other in (partner, cross, diag):
        pl.semaphore_signal(barrier, inc=1, device_id=(me, other),
                            device_id_type=pl.DeviceIdType.MESH)

    gpk[...] = jnp.zeros_like(gpk)
    gpk[0:1, 0:shard] = gain_a[...].astype(f32)
    gpk[1:2, 0:shard] = gain_m[...].astype(f32)
    gbuf[me] = gpk[...]
    own = [w_qkv[i] for i in range(3)] + [w_out[...].astype(f32).T.astype(bf16)]
    pa[me] = jnp.concatenate(own, axis=1)
    blank = jnp.zeros((shard, ffp - ff), bf16)
    pb[me] = jnp.concatenate(
        [w_in[0], blank, w_in[1], blank, w_down[...].astype(f32).T.astype(bf16), blank], axis=1)
    cbuf[t] = cotangent[...]

    pl.semaphore_wait(barrier, dp - 1 + 3)

    zc = lax.div(me, 2)
    yc = lax.rem(me, 2)
    deep = dp // 2
    beside = zc * 2 + (1 - yc)

    def column(i, y):
        return lax.rem(zc + i, deep) * 2 + y

    def gather_dp(buf):
        slots = [slot() for _ in range(dp - 1)]
        send(buf.at[me], buf.at[me], slots[0], beside, t)
        for i in range(1, deep):
            send(buf.at[me], buf.at[me], slots[i], column(i, yc), t)
        return slots

    def gather_dp_pass(buf, slots):
        for i in range(1, deep):
            origin = column(deep - i, yc)
            remote(buf.at[origin], buf.at[origin], slots[i], origin, t).wait_recv()
            send(buf.at[origin], buf.at[origin], slots[deep - 1 + i], beside, t)

    def gather_dp_end(buf, slots):
        remote(buf.at[beside], buf.at[beside], slots[0], beside, t).wait_recv()
        for i in range(1, deep):
            origin = column(deep - i, 1 - yc)
            remote(buf.at[origin], buf.at[origin], slots[deep - 1 + i], beside, t).wait_recv()

    def reduce_start(buf, over_y):
        slots = [slot() for _ in range(dp - 1)]
        for i in (*range(1, deep), 0):
            send(buf.at[column(i, 1 - yc)], over_y.at[i], slots[i], beside, t)
        return slots

    def reduce_pass(buf, over_y, over_z, slots):
        for i in range(1, deep):
            to = column(i, yc)
            remote(buf.at[to], over_y.at[i], slots[i], beside, t).wait_recv()
            buf[to] = (buf[to].astype(f32) + over_y[i].astype(f32)).astype(bf16)
            send(buf.at[to], over_z.at[i], slots[deep - 1 + i], to, t)

    def reduce_end(buf, over_y, over_z, slots):
        remote(buf.at[me], over_y.at[0], slots[0], beside, t).wait_recv()
        total = buf[me].astype(f32) + over_y[0].astype(f32)
        for i in range(1, deep):
            origin = column(deep - i, yc)
            remote(buf.at[origin], over_z.at[i], slots[deep - 1 + i], origin, t).wait_recv()
            total = total + over_z[i].astype(f32)
        return total

    def gather_small(buf):
        slots = []
        for i in range(1, dp):
            k = slot()
            slots.append(k)
            send(buf.at[me], buf.at[me], k, lax.rem(me + i, dp), t)
        return slots

    def gather_small_wait(buf, slots):
        for i in range(1, dp):
            origin = lax.rem(me + dp - i, dp)
            remote(buf.at[origin], buf.at[origin], slots[i - 1], origin, t).wait_recv()

    def rows_start(buf):
        slots = [slot(), slot(), slot()]
        send(buf.at[t], buf.at[t], slots[1], me, cross)
        send(buf.at[t], buf.at[t], slots[0], me, partner)
        return slots

    def rows_partner(buf, slots):
        remote(buf.at[partner], buf.at[partner], slots[0], me, partner).wait_recv()

    def rows_cross(buf, slots):
        remote(buf.at[cross], buf.at[cross], slots[1], me, cross).wait_recv()
        send(buf.at[cross], buf.at[cross], slots[2], me, partner)

    def rows_diag(buf, slots):
        remote(buf.at[diag], buf.at[diag], slots[2], me, partner).wait_recv()

    def sum_init(n):
        return (n, [slot(), slot(), slot()])

    def sum_diag(state, value):
        n, k = state
        s1[n, 0] = value.astype(bf16)
        send(s1.at[n, 0], r1.at[n, 0], k[0], me, partner)

    def sum_partner(state, value):
        n, k = state
        s1[n, 1] = value.astype(bf16)
        send(s1.at[n, 1], r1.at[n, 1], k[1], me, partner)

    def sum_cross(state, value):
        n, k = state
        remote(s1.at[n, 0], r1.at[n, 0], k[0], me, partner).wait_recv()
        s2[n] = (value + r1[n, 0].astype(f32)).astype(bf16)
        send(s2.at[n], r2.at[n], k[2], me, cross)

    def sum_own(state):
        n, k = state
        remote(s1.at[n, 1], r1.at[n, 1], k[1], me, partner).wait_recv()
        remote(s2.at[n], r2.at[n], k[2], me, cross).wait_recv()
        return r1[n, 1].astype(f32) + r2[n].astype(f32)

    def norm_parts(value):
        centred = value - jnp.mean(value, axis=-1, keepdims=True)
        spread = jnp.mean(centred * centred, axis=-1, keepdims=True)
        inverse = lax.rsqrt(spread + epsilon)
        return centred * inverse, inverse

    def norm_back(grad, gain, unit, inverse):
        scaled = grad * gain
        first = jnp.mean(scaled, axis=-1, keepdims=True)
        second = jnp.mean(scaled * unit, axis=-1, keepdims=True)
        return (inverse * (scaled - first - unit * second),
                jnp.sum(grad * unit, axis=0, keepdims=True))

    lanes = lax.broadcasted_iota(jnp.int32, (rows, 2 * width), 1)
    low_half = lax.rem(lanes, HEAD) < HEAD // 2

    def turn(value, b, sign):
        other = jnp.where(low_half, pltpu.roll(value, 2 * width - HEAD // 2, 1),
                          pltpu.roll(value, HEAD // 2, 1))
        times = 2 * width // 128
        cosine = jnp.concatenate([cos_t[b]] * times, axis=1)
        sine = jnp.concatenate([sin_t[b]] * times, axis=1)
        return value * cosine + sign * (other * sine)

    heads = width // HEAD
    scale = HEAD ** -0.5

    gain_slots = gather_small(gbuf)
    pa_slots = gather_dp(pa)
    unit, inverse1 = norm_parts(tokens[...].astype(f32))
    xh1[...] = unit
    gather_small_wait(gbuf, gain_slots)
    gain1 = jnp.concatenate([gbuf[j, 0:1, 0:shard] for j in range(dp)], axis=1)
    gain2 = jnp.concatenate([gbuf[j, 1:2, 0:shard] for j in range(dp)], axis=1)
    nbuf[t] = (unit * gain1).astype(bf16)
    n_slots = rows_start(nbuf)
    c_slots = rows_start(cbuf)
    gather_dp_pass(pa, pa_slots)
    gather_dp_end(pa, pa_slots)
    pb_slots = gather_dp(pb)
    wot[...] = pa[...].reshape(model, 4 * width)[:, 3 * width:]
    head_of = lax.div(lax.broadcasted_iota(jnp.int32, (rows, width), 1), HEAD)

    def project(b):
        proj = mm(nbuf[b], pa[...].reshape(model, 4 * width)[:, : 3 * width])
        turned = turn(proj[:, : 2 * width], b, 1.0)
        q = turned[:, :width]
        kk = turned[:, width:]
        vv = proj[:, 2 * width:]
        qs[b] = q.astype(bf16)
        qt[b] = q.T.astype(bf16)
        place = pl.ds(pl.multiple_of(b * rows, rows), rows)
        for h in range(heads):
            km[h, place, :] = jnp.where(head_of == h, kk, 0.0).astype(bf16)
            vm[h, place, :] = jnp.where(head_of == h, vv, 0.0).astype(bf16)

    project(t)
    rows_partner(nbuf, n_slots)
    project(partner)
    rows_cross(nbuf, n_slots)
    project(cross)
    rows_diag(nbuf, n_slots)
    project(diag)

    def attend(i):
        q = qs[i]
        acc = jnp.zeros((rows, width), f32)
        for h in range(heads):
            s = mm_nt(q, km[h]) * scale
            e = jnp.exp(s - jnp.max(s, axis=-1, keepdims=True))
            p = e * (1.0 / jnp.sum(e, axis=-1, keepdims=True))
            probs[h, i] = p
            acc = acc + mm(p.astype(bf16), vm[h])
        att[i] = acc.astype(bf16)

    def attend_two(first, second):
        def step(i, carry):
            attend(first + i * (second - first))
            return carry

        lax.fori_loop(0, 2, step, 0)

    st = sum_init(0)
    attend_two(diag, cross)
    sum_diag(st, mm_nt(att[diag], wot[...]))
    sum_cross(st, mm_nt(att[cross], wot[...]))
    attend_two(partner, t)
    sum_partner(st, mm_nt(att[partner], wot[...]))
    keep[0] = mm_nt(att[t], wot[...])
    gather_dp_pass(pb, pb_slots)
    rows_cross(cbuf, c_slots)
    rows_partner(cbuf, c_slots)
    rows_diag(cbuf, c_slots)
    res[...] = tokens[...].astype(f32) + (keep[0] + sum_own(st))
    unit2, inverse2 = norm_parts(res[...])
    xh2[...] = unit2
    mbuf[t] = (unit2 * gain2).astype(bf16)
    m_slots = rows_start(mbuf)
    gather_dp_end(pb, pb_slots)
    everything = pb[...].reshape(model, 3 * ffp)
    wgu[...] = everything[:, : 2 * ffp]
    wdt[...] = everything[:, 2 * ffp:]

    def mlp(b):
        gu = mm(mbuf[b], wgu[...])
        gate = gu[:, :ffp]
        up = gu[:, ffp:]
        phi = 0.5 * (1.0 + lax.erf(gate * 0.7071067811865476))
        act = gate * phi
        hid[b] = (act * up).astype(bf16)
        gh = mm(cbuf[b], wdt[...])
        slope = phi + gate * (jnp.exp(-0.5 * gate * gate) * 0.3989422804014327)
        ggu[b, :, :ffp] = (gh * up * slope).astype(bf16)
        ggu[b, :, ffp:] = (gh * act).astype(bf16)

    st_g = sum_init(1)
    mlp(t)
    keep[0] = mm_nt(ggu[t], wgu[...])
    rows_partner(mbuf, m_slots)
    mlp(partner)
    sum_partner(st_g, mm_nt(ggu[partner], wgu[...]))
    rows_cross(mbuf, m_slots)
    rows_diag(mbuf, m_slots)
    mlp(diag)
    sum_diag(st_g, mm_nt(ggu[diag], wgu[...]))
    mlp(cross)
    sum_cross(st_g, mm_nt(ggu[cross], wgu[...]))

    mflat = mbuf[...].reshape(group, model)

    def reduce_small(buf, received):
        slots = []
        for i in range(1, dp):
            k = slot()
            slots.append(k)
            peer = lax.rem(me + i, dp)
            send(buf.at[peer], received.at[me], k, peer, t)
        return slots

    def reduce_small_wait(buf, received, slots):
        total = buf[me].astype(f32)
        for i in range(1, dp):
            origin = lax.rem(me + dp - i, dp)
            remote(buf.at[origin], received.at[origin], slots[i - 1], origin, t).wait_recv()
            total = total + received[origin].astype(f32)
        return total

    for part in range(2):
        cut = slice(part * ffp, (part + 1) * ffp)
        piece = mm_tn(mflat, ggu[:, :, cut].reshape(group, ffp))
        gb_s[:, :, cut] = piece.astype(bf16).reshape(dp, shard, ffp)
    gb_slots = reduce_start(gb_s, gb_y)

    gnm = keep[0] + sum_own(st_g)
    back2, ggm = norm_back(gnm, gain2, xh2[...], inverse2)
    gmix[...] = cotangent[...].astype(f32) + back2
    bbuf[t] = gmix[...].astype(bf16)
    b_slots = rows_start(bbuf)

    st_d = sum_init(2)
    sum_diag(st_d, mm_nt(hid[diag], wdt[...]))
    sum_partner(st_d, mm_nt(hid[partner], wdt[...]))
    piece = mm_tn(cbuf[...].reshape(group, model), hid[...].reshape(group, ffp))
    gf_s[...] = piece.astype(bf16).reshape(dp, shard, ffp)
    gf_slots = reduce_start(gf_s, gf_y)
    rows_cross(bbuf, b_slots)
    sum_cross(st_d, mm_nt(hid[cross], wdt[...]))
    keep[0] = mm_nt(hid[t], wdt[...])
    rows_partner(bbuf, b_slots)
    rows_diag(bbuf, b_slots)

    piece = mm_tn(bbuf[...].reshape(group, model), att[...].reshape(group, width))
    go_s[...] = piece.astype(bf16).reshape(dp, shard, width)
    go_slots = reduce_start(go_s, go_y)
    reduce_pass(gb_s, gb_y, gb_z, gb_slots)
    gkt[...] = jnp.zeros_like(gkt)
    gvt[...] = jnp.zeros_like(gvt)

    def attend_back(i, carry):
        ga = mm(bbuf[i], wot[...])
        gab = ga.astype(bf16)
        gatt[i] = gab
        gat = ga.T.astype(bf16)
        acc = jnp.zeros((rows, width), f32)
        for h in range(heads):
            some = slice(h * HEAD, (h + 1) * HEAD)
            gp = mm_nt(gab, vm[h])
            p = probs[h, i]
            inner = jnp.sum(p * gp, axis=-1, keepdims=True)
            gs = (p * (gp - inner)).astype(bf16)
            acc = acc + mm(gs, km[h])
            gkt[some, :] += mm(qt[i, some, :], gs)
            gvt[some, :] += mm(gat[some, :], p.astype(bf16))
        gqs[i] = acc * scale
        return carry

    lax.fori_loop(0, 4, attend_back, 0)

    def join(b, carry):
        place = pl.ds(pl.multiple_of(b * rows, rows), rows)
        gk = gkt[:, place].T * scale
        back = turn(jnp.concatenate([gqs[b], gk], axis=1), b, -1.0)
        gproj[b, :, : 2 * width] = back.astype(bf16)
        gproj[b, :, 2 * width:] = gvt[:, place].T.astype(bf16)
        return carry

    lax.fori_loop(0, 4, join, 0)
    reduce_pass(gf_s, gf_y, gf_z, gf_slots)
    reduce_pass(go_s, go_y, go_z, go_slots)
    wqkv = pa[...].reshape(model, 4 * width)[:, : 3 * width]
    mixed[...] = (res[...] + (keep[0] + sum_own(st_d))).astype(bf16)
    st_a = sum_init(3)
    sum_diag(st_a, mm_nt(gproj[diag], wqkv))
    sum_partner(st_a, mm_nt(gproj[partner], wqkv))
    sum_cross(st_a, mm_nt(gproj[cross], wqkv))
    piece = mm_tn(nbuf[...].reshape(group, model), gproj[...].reshape(group, 3 * width))
    ga_s[...] = piece.astype(bf16).reshape(dp, shard, 3 * width)
    ga_slots = reduce_start(ga_s, ga_y)
    keep[0] = mm_nt(gproj[t], wqkv)

    total = reduce_end(gb_s, gb_y, gb_z, gb_slots)
    gin_out[0] = total[:, :ff]
    gin_out[1] = total[:, ffp: ffp + ff]
    reduce_pass(ga_s, ga_y, ga_z, ga_slots)
    total = reduce_end(gf_s, gf_y, gf_z, gf_slots)
    gdown_out[...] = total.T[:ff]
    total = reduce_end(go_s, go_y, go_z, go_slots)
    gout_out[...] = total.T

    gna = keep[0] + sum_own(st_a)
    back1, gga = norm_back(gna, gain1, xh1[...], inverse1)
    gt[t] = jnp.concatenate([gga, ggm, jnp.zeros((6, model), f32)], axis=0)
    tslots = [slot(), slot(), slot()]
    for k, other in zip(tslots, (partner, cross, diag)):
        send(gt.at[t], gt.at[t], k, me, other)
    input_grad[...] = gmix[...] + back1
    for k, other in zip(tslots, (partner, cross, diag)):
        remote(gt.at[other], gt.at[other], k, me, other).wait_recv()
    gains = (gt[0] + gt[1]) + (gt[2] + gt[3])
    for j in range(dp):
        gd_s[j, :, 0:shard] = gains[:, j * shard:(j + 1) * shard]
        gd_s[j, :, shard:] = jnp.zeros((8, 128 - shard), f32)
    gd_slots = reduce_small(gd_s, gd_r)
    total = reduce_end(ga_s, ga_y, ga_z, ga_slots)
    for i in range(3):
        gqkv_out[i] = total[:, i * width:(i + 1) * width]
    total = reduce_small_wait(gd_s, gd_r, gd_slots)
    gga_out[...] = total[0:1, :shard]
    ggm_out[...] = total[1:2, :shard]
    for copy in sent:
        copy.wait_send()


def move_kernel(*refs):
    for i in range(8):
        refs[8 + i][...] = refs[i][...]


def per_device(tokens, gain_attn, gain_mlp, w_qkv, w_out, w_in, w_down, cotangent):
    dp = lax.axis_size("dp")
    rows, model = tokens.shape
    shard, width = w_qkv.shape[1:]
    ff = w_in.shape[2]
    one_sequence = lax.axis_size("tensor") == 4 and rows * 4 == LEN
    if not (one_sequence and dp == 8 and shard % 16 == 0 and shard <= 128 and 2 * width % 128 == 0):
        return plain_layer(tokens, gain_attn, gain_mlp, w_qkv, w_out, w_in, w_down, cotangent)
    ffp = -(-ff // 128) * 128
    half = np.arange(HEAD // 2, dtype=np.float32)
    frequency = np.float32(rope_base) ** (np.float32(-2.0) * half / np.float32(HEAD))
    angles = np.arange(LEN, dtype=np.float32)[:, None] * frequency[None, :].astype(np.float32)
    cosine, sine = np.cos(angles), np.sin(angles)
    cos_t = np.concatenate([cosine] * 4, axis=1).reshape(4, rows, 2 * HEAD)
    sin_t = np.concatenate([-sine, sine] * 2, axis=1).reshape(4, rows, 2 * HEAD)
    vmem = pltpu.VMEM

    def reduction(columns):
        return [vmem((count, shard, columns), bf16) for count in (dp, dp // 2, dp // 2)]

    scratch = [
        vmem((8, 128), f32), vmem((dp, 8, 128), f32),
        vmem((dp, shard, 4 * width), bf16), vmem((dp, shard, 3 * ffp), bf16),
        vmem((4, rows, model), bf16), vmem((4, rows, model), bf16),
        vmem((4, rows, model), bf16), vmem((4, rows, model), bf16),
        vmem((model, 2 * ffp), bf16), vmem((model, ffp), bf16), vmem((model, width), bf16),
        vmem((4, rows, width), bf16), vmem((4, width, rows), bf16),
        vmem((width // HEAD, LEN, width), bf16), vmem((width // HEAD, LEN, width), bf16),
        vmem((width // HEAD, 4, rows, LEN), f32),
        vmem((4, rows, width), bf16), vmem((4, rows, width), bf16),
        vmem((4, rows, 3 * width), bf16), vmem((4, rows, width), f32),
        vmem((width, LEN), f32), vmem((width, LEN), f32),
        vmem((4, rows, ffp), bf16), vmem((4, rows, 2 * ffp), bf16),
        vmem((rows, model), f32), vmem((rows, model), f32),
        vmem((rows, model), f32), vmem((rows, model), f32), vmem((1, rows, model), f32),
        vmem((4, 2, rows, model), bf16), vmem((4, 2, rows, model), bf16),
        vmem((4, rows, model), bf16), vmem((4, rows, model), bf16),
        *reduction(3 * width), *reduction(width), *reduction(2 * ffp), *reduction(ffp),
        vmem((4, 8, model), f32), vmem((dp, 8, 128), f32), vmem((dp, 8, 128), f32),
        pltpu.SemaphoreType.DMA((8 * (dp - 1) + 27,)),
        pltpu.SemaphoreType.DMA((8 * (dp - 1) + 27,)),
    ]
    whole = pl.BlockSpec(memory_space=pltpu.VMEM)
    shape = jax.ShapeDtypeStruct
    outs = pl.pallas_call(
        functools.partial(layer_kernel, dp, rows, width, ff, ffp),
        out_shape=[
            shape((rows, model), bf16), shape((rows, model), f32),
            shape((1, shard), f32), shape((1, shard), f32),
            shape(w_qkv.shape, f32), shape(w_out.shape, f32),
            shape(w_in.shape, f32), shape(w_down.shape, f32),
        ],
        in_specs=[whole] * 10,
        out_specs=[whole] * 8,
        scratch_shapes=scratch,
        compiler_params=pltpu.CompilerParams(
            collective_id=0, has_side_effects=True, vmem_limit_bytes=62 * 1024 * 1024),
    )(tokens, gain_attn[None], gain_mlp[None], w_qkv, w_out, w_in, w_down, cotangent, cos_t, sin_t)
    outs = pl.pallas_call(
        move_kernel,
        out_shape=[shape(o.shape, o.dtype) for o in outs],
        in_specs=[whole] * 8,
        out_specs=[whole] * 8,
    )(*outs)
    mixed, input_grad, gga, ggm, gqkv, gout, gin, gdown = outs
    return mixed, input_grad, gga[0], ggm[0], gqkv, gout, gin, gdown


def solution(mesh):
    placed = (
        P(("dp", "tensor"), None),
        P("dp"),
        P("dp"),
        P(None, "dp", "tensor"),
        P("tensor", "dp"),
        P(None, "dp", "tensor"),
        P("tensor", "dp"),
        P(("dp", "tensor"), None),
    )
    return jax.shard_map(
        per_device,
        mesh=mesh,
        in_specs=placed,
        out_specs=(
            P(("dp", "tensor"), None),
            P(("dp", "tensor"), None),
            P("dp"),
            P("dp"),
            P(None, "dp", "tensor"),
            P("tensor", "dp"),
            P(None, "dp", "tensor"),
            P("tensor", "dp"),
        ),
        check_vma=False,
    )
```
